32 devices in a mesh: groups: 2 (over x), ctx: 16 (over z, y, core).
Axes of the slice: x: 2, y: 2, z: 4, core: 2. Of those that a mesh axis runs over, the one named last changes fastest.
Arguments:
- values: bfloat16 [4096, 4096], P(('groups', 'ctx')), parts along dimension 0, may hold values from -6 to 6
- in_b: bfloat16 [4096, 512], P(('groups', 'ctx')), parts along dimension 0, may hold values from -0.75 to 0.75
- out_c: bfloat16 [4096, 512], P(('groups', 'ctx')), parts along dimension 0, may hold values from -6 to 6
- decay_log: float32 [64, 4096], P(None, ('groups', 'ctx')), parts along dimension 1, may hold values from -1 to 0
- residual: bfloat16 [4096, 4096], P(('groups', 'ctx')), parts along dimension 0, may hold values from -40 to 40
- mixer_gain: float32 [4096], replicated, may hold values from 0.5 to 1.5
- moe_gain: float32 [4096], replicated, may hold values from 0.5 to 1.5
- w_down: bfloat16 [4096, 1024], P('ctx'), may hold values from -0.09375 to 0.09375
- w_in: bfloat16 [16, 1024, 1024], P('ctx'), may hold values from -0.1875 to 0.1875
- w_out: bfloat16 [16, 1024, 1024], P('ctx'), may hold values from -0.1875 to 0.1875
- routes: int32 [4096, 6], P(('groups', 'ctx')), parts along dimension 0, may hold values from 0 to 15, all different within a row; in each aligned block of 128 rows (0 to 127, 128 to 255, ...) at most 72 rows name the same one
- gate_int: int32 [4096, 6], P(('groups', 'ctx')), parts along dimension 0, may hold values from 1 to 16
Outputs:
- mixed: bfloat16 [4096, 4096], P(('groups', 'ctx')), parts along dimension 0
- latent_mix: bfloat16 [4096, 1024], P(('groups', 'ctx')), parts along dimension 0
The draws below stay inside these ranges and needn't reach their ends.
There are 2 independent parts, one for each index of `groups`. The reference program is written for one: setup_inputs(seed, part) draws one part's arguments, and reference() takes and returns one part's arrays. A program takes and returns all parts, laid end to end along the dimension named above; an argument that names none is the same for every part. Nothing has to cross between parts.
Inputs may be any that keep to these rules, and one draw needn't show every extreme that they name: `routes`: each row names 6 different experts; within the 128 rows of one device, no expert is named more than 72 times, a bound that some block reaches.
All inputs are finite; a program needn't handle non-finite values.
Results may differ from the reference program's by a relative error of at most 0.013.
Values may be sent and summed in bfloat16 or wider, within the bound.
A program may use at most 320 MiB of HBM per device.

```python
import math
import jax
import jax.numpy as jnp
import numpy as np
from jax import lax

D = 4096
MIXER_HEADS = 64
P_SIZE = 64
N = 64
GROUPS = 8
L = 1024
FFE = 1024
TOPK = 6
BLOCK = 128
TOK_DEV = 128
EXPERTS = 16
SEQUENCE_TOKENS = 2048
CAP = 72
N_CTX = 16


def draw_decay_log(key, part):
    key = jax.random.fold_in(key, 11)
    random_keys = jax.random.split(key, 7)
    fast_share = 0.5
    fast_heads = jax.random.uniform(random_keys[0], (MIXER_HEADS,)) < fast_share
    fast_rate = 1.0 / jax.random.uniform(random_keys[1], (MIXER_HEADS,), jnp.float32, 30.0, 50.0)
    slow_rate = jax.random.uniform(random_keys[2], (MIXER_HEADS,), jnp.float32, 0.1, 0.6) / SEQUENCE_TOKENS
    head_rate_value = jnp.where(fast_heads, fast_rate, slow_rate)
    shard_multiplier = jnp.exp(jax.random.uniform(random_keys[3], (MIXER_HEADS, SEQUENCE_TOKENS // TOK_DEV), jnp.float32, -0.7, 0.7))
    shard_multiplier = jnp.repeat(shard_multiplier, TOK_DEV, axis=1)
    jaggedness = jax.random.uniform(random_keys[4], (MIXER_HEADS, SEQUENCE_TOKENS), jnp.float32, 0.5, 1.5)
    spike_position = jax.random.randint(random_keys[5], (2,), 0, SEQUENCE_TOKENS)
    token_position = jnp.arange(SEQUENCE_TOKENS)
    spike_reached = (token_position == spike_position[0]) | (token_position == spike_position[1])
    spike_penalty = jax.random.uniform(random_keys[6], (MIXER_HEADS, SEQUENCE_TOKENS), jnp.float32, 0.2, 0.5)
    final_output = -head_rate_value[:, None] * shard_multiplier * jaggedness + jnp.where(spike_reached[None, :], jnp.log(1.0 - spike_penalty), 0.0)
    return final_output.astype(jnp.float32)


def draw_residual(key, part):
    key = jax.random.fold_in(key, 23)
    random_keys = jax.random.split(key, 3)
    row_scale = 10.0 ** jax.random.uniform(random_keys[0], (SEQUENCE_TOKENS, 1), jnp.float32, -0.5, 0.5)
    column_scale = 10.0 ** jax.random.uniform(random_keys[1], (1, D), jnp.float32, -0.5, 0.5)
    base = jnp.clip(jax.random.normal(random_keys[2], (SEQUENCE_TOKENS, D), jnp.float32), -4.0, 4.0)
    return (base * row_scale * column_scale).astype(jnp.bfloat16)


def touch_ends(array, stream_key, smallest, high):
    place = [jax.random.randint(jax.random.fold_in(stream_key, axis), (), 0, length) for axis, length in enumerate(array.shape)]
    longest = array.shape.index(max(array.shape))
    beside = place[:longest] + [(place[longest] + 1) % array.shape[longest]] + place[longest + 1:]
    return array.at[tuple(place)].set(smallest).at[tuple(beside)].set(high)


def block_scale(own_key, extent, pieces, low, top_value):
    def one(dim, parts):
        heights = jax.random.uniform(jax.random.fold_in(jax.random.fold_in(own_key, 6), dim), (parts,), jnp.float32, low / len(pieces), top_value / len(pieces))
        return jnp.repeat(jnp.exp(heights), extent[dim] // parts).reshape((-1,) + (1,) * (len(extent) - dim - 1))

    gain = one(*pieces[0])
    for cut in pieces[1:]:
        gain = gain * one(*cut)
    return gain


def shared_out(stream_key, own, number, rows, number_of, top, bound, skew):
    order = jax.random.permutation(stream_key, number_of)
    crowded, ordinary = shares(number_of, rows * top, bound, skew, True), shares(number_of, rows * top, bound, skew, False)
    places = jnp.arange(number_of)

    def named(sizes, turn):
        used = int((sizes > 0).sum())
        fixed = max(1, used // 4)
        shifted = fixed + (places - fixed + turn * (used - fixed)) % max(1, number_of - fixed)
        return jnp.zeros((number_of,), jnp.int32).at[order[jnp.where(places < fixed, places, shifted)]].set(jnp.asarray(sizes, jnp.int32))

    sizes = jnp.where(number % 4 == 0, named(crowded, number // 4), named(ordinary, number - number // 4 - 1))
    mixed = jax.random.permutation(jax.random.fold_in(own, 3), number_of)
    giver, receiver = mixed[0:number_of // 2 * 2:2], mixed[1:number_of // 2 * 2:2]
    margin = jnp.minimum(sizes[giver] - 1, bound - sizes[receiver]) // 2
    margin = jnp.where((giver == order[0]) | (receiver == order[0]) | (sizes[receiver] == 0), 0, jnp.maximum(margin, 0))
    shifted = jax.random.randint(jax.random.fold_in(own, 4), (number_of // 2,), 0, 1 << 20) % (margin + 1)
    sizes = sizes.at[giver].add(-shifted).at[receiver].add(shifted)
    items = jnp.searchsorted(jnp.cumsum(sizes), jnp.arange(rows * top), side="right").astype(jnp.int32)
    table = items.reshape(top, rows).T
    table = table[jax.random.permutation(jax.random.fold_in(own, 1), rows)]
    turn = jax.random.randint(jax.random.fold_in(own, 2), (rows, 1), 0, top)
    return jnp.take_along_axis(table, (jnp.arange(top)[None, :] + turn) % top, axis=1)


def shares(amount, total, limit, slope, full):
    loads = [(1 << 20) // math.isqrt(rank ** slope) + 1 for rank in range(1, amount + 1)]
    largest = limit if full else min(limit, max(-(-total // amount), total * loads[0] // sum(loads)))
    least = 1 if total - largest >= amount - 1 else 0
    holding, spare = [largest] + [least] * (amount - 1), total - largest - least * (amount - 1)
    while spare > 0:
        candidates = [i for i in range(1, amount) if holding[i] < largest] or [i for i in range(1, amount) if holding[i] < limit]
        whole, remaining = sum([loads[i] for i in candidates]), spare
        for i in candidates:
            more = min(limit - holding[i], max(1, remaining * loads[i] // whole), spare)
            holding[i] = holding[i] + more
            spare = spare - more
    return np.array(holding)


def bell_draw(key, extent, scale, most, cuts=(), held_as=jnp.bfloat16):
    drawn = scale * jax.random.normal(key, extent, jnp.float32)
    if cuts:
        drawn = drawn * block_scale(key, extent, cuts, -0.22, 0.18)
    return jnp.clip(drawn, -most, most).astype(held_as)


def setup_inputs(seed: int = 0, part: int = 0) -> dict:
    splits = jax.random.split(jax.random.key(seed), 13)
    own_keys = jax.random.split(jax.random.fold_in(splits[12], part), 13)
    values = bell_draw(own_keys[0], (SEQUENCE_TOKENS, D), 1.0, 6.0, ((0, 16),))
    in_b = bell_draw(own_keys[1], (SEQUENCE_TOKENS, GROUPS * N), N ** -0.5, 0.75, ((0, 16),))
    out_c = bell_draw(own_keys[2], (SEQUENCE_TOKENS, GROUPS * N), 1.0, 6.0, ((0, 16),))
    decay_log = draw_decay_log(jax.random.fold_in(jax.random.fold_in(splits[12], part), 71), part)
    residual = draw_residual(jax.random.fold_in(jax.random.fold_in(splits[12], part), 71), part)
    mixer_gain = jnp.clip(1.0 + 0.1 * jax.random.normal(splits[5], (D,), jnp.float32), 0.5, 1.5)
    moe_gain = jnp.clip(1.0 + 0.1 * jax.random.normal(splits[6], (D,), jnp.float32), 0.5, 1.5)
    w_down = bell_draw(splits[7], (D, L), D ** -0.5, 0.09375, ((0, 16),))
    w_in = bell_draw(splits[8], (EXPERTS, L, FFE), L ** -0.5, 0.1875, ((0, 16),))
    w_out = bell_draw(splits[9], (EXPERTS, FFE, L), FFE ** -0.5, 0.1875, ((0, 16),))
    routes_keys = jax.random.split(jax.random.fold_in(own_keys[10], 1), SEQUENCE_TOKENS // TOK_DEV)
    routes_turns = jax.random.permutation(jax.random.fold_in(own_keys[10], 3), SEQUENCE_TOKENS // TOK_DEV)
    routes = jax.vmap(lambda own, number: shared_out(jax.random.fold_in(own_keys[10], 2), own, number, TOK_DEV, EXPERTS, TOPK, CAP, 1))(routes_keys, routes_turns).reshape((SEQUENCE_TOKENS, TOPK))
    gate_int = touch_ends(jax.random.randint(own_keys[11], (SEQUENCE_TOKENS, TOPK), 1, 17), jax.random.fold_in(own_keys[11], 1), 1, 16).astype(jnp.int32)
    return dict(values=values, in_b=in_b, out_c=out_c, decay_log=decay_log, residual=residual, mixer_gain=mixer_gain, moe_gain=moe_gain, w_down=w_down, w_in=w_in, w_out=w_out, routes=routes, gate_int=gate_int)


def block_terms(block_values, block_in, block_out, block_logs):
    running = jnp.cumsum(block_logs, axis=-1)
    scores = jnp.einsum('tgn,sgn->gts', block_out.astype(jnp.float32), block_in.astype(jnp.float32))
    length = block_logs.shape[-1]
    lower = jnp.arange(length)[:, None] >= jnp.arange(length)[None, :]
    spread = running[..., :, None] - running[..., None, :]
    decays = jnp.where(lower, jnp.exp(jnp.where(lower, spread, 0.0)), 0.0)
    weights = (scores[:, None] * decays).astype(jnp.bfloat16)
    inner = jnp.einsum('ghts,sghp->tghp', weights.astype(jnp.float32), block_values.astype(jnp.float32))
    tails = jnp.exp(running[..., -1:] - running)
    scaled = (block_values.astype(jnp.float32) * jnp.transpose(tails, (2, 0, 1))[..., None]).astype(jnp.bfloat16)
    update = jnp.einsum('sghp,sgn->ghpn', scaled.astype(jnp.float32), block_in.astype(jnp.float32))
    return (running, inner, update)

def carry_term(running, block_out, carried):
    reach = jnp.einsum('tgn,ghpn->tghp', block_out.astype(jnp.float32), carried, precision=lax.Precision.HIGHEST)
    return jnp.transpose(jnp.exp(running), (2, 0, 1))[..., None] * reach

def reference(values, in_b, out_c, decay_log, residual, mixer_gain, moe_gain, w_down, w_in, w_out, routes, gate_int):
    per_group = MIXER_HEADS // GROUPS
    blocks = SEQUENCE_TOKENS // BLOCK
    value_blocks = values.reshape(blocks, BLOCK, GROUPS, per_group, P_SIZE)
    in_blocks = in_b.reshape(blocks, BLOCK, GROUPS, N)
    out_blocks = out_c.reshape(blocks, BLOCK, GROUPS, N)
    log_blocks = jnp.transpose(decay_log.reshape(GROUPS, per_group, blocks, BLOCK), (2, 0, 1, 3))

    def advance(carried, block_args):
        block_values, block_in, block_out, block_logs = block_args
        running, inner, update = block_terms(block_values, block_in, block_out, block_logs)
        output = inner + carry_term(running, block_out, carried)
        carried = jnp.exp(running[..., -1])[..., None, None] * carried + update
        return (carried, output)
    start_state = jnp.zeros((GROUPS, per_group, P_SIZE, N), jnp.float32)
    _, outputs = lax.scan(advance, start_state, (value_blocks, in_blocks, out_blocks, log_blocks))
    heads_out = outputs.reshape(SEQUENCE_TOKENS, MIXER_HEADS, P_SIZE)
    scale = lax.rsqrt(lax.optimization_barrier(jnp.mean(heads_out * heads_out, axis=-1, keepdims=True)) + 1e-05)
    normed_heads = (heads_out * scale * mixer_gain.reshape(MIXER_HEADS, P_SIZE)).reshape(SEQUENCE_TOKENS, D)
    mixed = (residual.astype(jnp.float32) + normed_heads).astype(jnp.bfloat16)
    wide = mixed.astype(jnp.float32)
    normed = (wide * lax.rsqrt(lax.optimization_barrier(jnp.mean(wide * wide, axis=-1, keepdims=True)) + 1e-05) * moe_gain).astype(jnp.bfloat16)
    latent = jnp.dot(normed, w_down, preferred_element_type=jnp.float32).astype(jnp.bfloat16)
    flat_routes = routes.reshape(N_CTX, TOK_DEV * TOPK)
    onehot = (flat_routes[..., None] == jnp.arange(EXPERTS, dtype=jnp.int32)).astype(jnp.int32)
    slot_index = lax.optimization_barrier(jnp.sum((jnp.cumsum(onehot, axis=1) - onehot) * onehot, axis=-1)).reshape(-1).astype(jnp.int32)
    source = (jnp.arange(SEQUENCE_TOKENS * TOPK, dtype=jnp.int32) // (TOK_DEV * TOPK)).astype(jnp.int32)
    expert_ids = routes.reshape(-1).astype(jnp.int32)
    positions = (source * CAP + slot_index).astype(jnp.int32)
    sent_rows = jnp.repeat(latent, TOPK, axis=0)
    buffers = jnp.zeros((EXPERTS, N_CTX * CAP, L), jnp.bfloat16).at[expert_ids, positions].set(sent_rows)

    def apply_expert(expert_args):
        rows, first, second = expert_args
        hidden_act = jnp.square(jax.nn.relu(jnp.dot(rows, first, preferred_element_type=jnp.float32))).astype(jnp.bfloat16)
        return jnp.dot(hidden_act, second, preferred_element_type=jnp.float32).astype(jnp.bfloat16)
    results = lax.map(apply_expert, (buffers, w_in, w_out))
    picked = results[expert_ids, positions].reshape(SEQUENCE_TOKENS, TOPK, L)
    gate_float = gate_int.astype(jnp.float32)
    gate = gate_float / lax.optimization_barrier(jnp.sum(gate_float, axis=1, keepdims=True))
    latent_mix = lax.optimization_barrier(jnp.sum(picked.astype(jnp.float32) * gate[..., None], axis=1)).astype(jnp.bfloat16)
    return (mixed, latent_mix)
```

```python
import functools

import jax
import jax.numpy as jnp
from jax import lax
from jax.experimental import pallas as pl
from jax.experimental.pallas import tpu as pltpu
from jax.sharding import PartitionSpec as P

P_SIZE = 64
N = 64
GROUPS = 8
EXTRA = 16
MESH = pl.DeviceIdType.MESH
F32 = jnp.float32
BF16 = jnp.bfloat16


def ring_place(chips, chip):
    if chips == 8:
        z, y = chip // 2, chip % 2
        return z * (1 - y) + (7 - z) * y
    return chip


def ring_chip(chips, place):
    place = lax.rem(place + 2 * chips, chips)
    if chips == 8:
        back = place // 4
        return (1 - back) * (2 * place) + back * (2 * (7 - place) + 1)
    return place


def remote(src, dst, send, recv, device):
    return pltpu.make_async_remote_copy(
        src_ref=src,
        dst_ref=dst,
        send_sem=send,
        recv_sem=recv,
        device_id={"ctx": device},
        device_id_type=MESH,
    )


class Gather:
    def __init__(self, buf, chips, place, core, sems):
        self.buf, self.chips, self.place, self.core = buf, chips, place, core
        self.half = chips // 2
        self.rows = buf.shape[1]
        self.ring_send, self.ring_recv, self.side_send, self.side_recv = sems
        self.started = []

    def slot(self, place, core=None):
        return ring_chip(self.chips, place) * 2 + (self.core if core is None else core)

    def part(self, place, way, step, core=None):
        block = self.buf.at[self.slot(place, core)]
        if step == self.half - 1:
            block = block.at[pl.ds(way * (self.rows // 2), self.rows // 2)]
        return block

    def ring(self, way, step):
        sign = 1 - 2 * way
        block = self.part(self.place - sign * step, way, step)
        return remote(
            block,
            block,
            self.ring_send.at[way * self.half + step],
            self.ring_recv.at[way * self.half + step],
            self.slot(self.place + sign),
        )

    def side(self, index, block):
        return remote(
            block,
            block,
            self.side_send.at[index],
            self.side_recv.at[index],
            self.slot(self.place, 1 - self.core),
        )

    def go(self, copy):
        copy.start()
        self.started.append(copy)

    def start(self):
        for way in range(2):
            self.go(self.ring(way, 0))
        self.go(self.side(0, self.buf.at[self.slot(self.place)]))

    def step(self, step):
        for way in range(2):
            sign = 1 - 2 * way
            came = self.part(self.place - sign * (step + 1), way, step)
            remote(
                came,
                came,
                self.ring_send.at[way * self.half + step],
                self.ring_recv.at[way * self.half + step],
                self.slot(self.place + sign),
            ).wait_recv()
            if step + 1 < self.half:
                self.go(self.ring(way, step + 1))
            self.go(self.side(1 + 2 * step + way, came))

    def wait_side(self, step):
        if step < 0:
            block = self.buf.at[self.slot(self.place, 1 - self.core)]
            self.side(0, block).wait_recv()
            return
        for way in range(2):
            sign = 1 - 2 * way
            block = self.part(self.place - sign * (step + 1), way, step, 1 - self.core)
            self.side(1 + 2 * step + way, block).wait_recv()

    def finish(self):
        for copy in self.started:
            copy.wait_send()
        self.started = []


def kernel(
    n,
    values,
    in_b,
    out_c,
    decay_log,
    residual,
    mixer_gain,
    moe_gain,
    gates,
    w_down,
    w_in,
    w_out,
    mixed_out,
    mix_out,
    w_buf,
    lat_buf,
    *rest,
):
    chips = n // 2
    half = chips // 2
    apart = n <= 16
    if apart:
        parts, rest = rest[0], rest[1:]
    else:
        parts = lat_buf
    (
        y_buf,
        logs_t,
        normed,
        acc,
        st_send,
        st_recv,
        st_back,
        st_enter,
        gate_buf,
        win_buf,
        wout_buf,
        side_parts,
        sums,
        half_sums,
        local_sem,
        st_sem,
        st_rsem,
        back_sem,
        back_rsem,
        gate_sem,
        gate_rsem,
        w_ring_s,
        w_ring_r,
        w_side_s,
        w_side_r,
        l_ring_s,
        l_ring_r,
        l_side_s,
        l_side_r,
        p_side_s,
        p_side_r,
        s_send,
        s_recv,
    ) = rest
    me = lax.axis_index("ctx")
    core = lax.rem(me, 2)
    place = ring_place(chips, me // 2)
    tok = values.shape[0]
    width = values.shape[1] // n

    load_down = pltpu.make_async_copy(w_down, w_buf.at[me], local_sem.at[0])
    load_in = pltpu.make_async_copy(w_in.at[0], win_buf, local_sem.at[1])
    load_out = pltpu.make_async_copy(w_out.at[0], wout_buf, local_sem.at[2])
    load_down.start()
    load_in.start()
    load_out.start()

    barrier = pltpu.get_barrier_semaphore()

    @pl.loop(1, n)
    def _(i):
        pl.semaphore_signal(
            barrier, inc=1, device_id={"ctx": lax.rem(me + i, n)}, device_id_type=MESH
        )

    pl.semaphore_wait(barrier, n - 1)
    load_down.wait()
    down = Gather(w_buf, chips, place, core, (w_ring_s, w_ring_r, w_side_s, w_side_r))
    down.start()

    def gate_copy(to):
        return remote(gates.at[to], gate_buf.at[me], gate_sem.at[to], gate_rsem.at[me], to)

    @pl.loop(1, n)
    def _(i):
        gate_copy(lax.rem(me + i, n)).start()

    gate_buf[me] = gates[me]

    row = lax.broadcasted_iota(jnp.int32, (tok, tok), 0)
    col = lax.broadcasted_iota(jnp.int32, (tok, tok), 1)
    lower = row >= col
    lower_f = lower.astype(F32)
    upper_f = (row <= col).astype(F32)
    left = lax.broadcasted_iota(jnp.int32, (tok, 128), 1) < P_SIZE
    left_row = left[:1]
    extra_row = lax.broadcasted_iota(jnp.int32, (EXTRA, 128), 0)

    def pair(a, b):
        return jnp.where(left, a, b)

    def st_copy(to):
        return remote(st_send.at[to], st_recv.at[me], st_sem.at[to], st_rsem.at[me], to)

    per_gp = n // 4

    @pl.loop(0, 4)
    def _(gp):
        logs = decay_log[pl.ds(pl.multiple_of(gp * 16, 16), 16), :]
        run = jnp.dot(logs, upper_f, precision=lax.Precision.HIGHEST, preferred_element_type=F32)
        run_t = lax.dot_general(
            lower_f,
            logs,
            (((1,), (1,)), ((), ())),
            precision=lax.Precision.HIGHEST,
            preferred_element_type=F32,
        )
        logs_t[gp] = run_t
        tails = jnp.exp(run_t[tok - 1 : tok, :] - run_t)
        total = jnp.exp(run_t[tok - 1 : tok, :])
        two = pl.ds(pl.multiple_of(gp * 128, 128), 128)
        b2, c2 = in_b[:, two], out_c[:, two]
        for gi in range(2):
            b = b2[:, gi * N : (gi + 1) * N]
            c = c2[:, gi * N : (gi + 1) * N]
            scores = lax.dot_general(c, b, (((1,), (1,)), ((), ())), preferred_element_type=F32)
            for hp in range(4):
                h = gi * 8 + hp * 2
                cols = pl.ds(pl.multiple_of(gp * 1024 + gi * 512 + hp * 128, 128), 128)
                v = values[:, cols]
                weights = []
                for k in range(2):
                    spread = run_t[:, h + k : h + k + 1] - run[h + k : h + k + 1, :]
                    decays = jnp.exp(jnp.where(lower, spread, -1e30))
                    weights.append((scores * decays).astype(BF16))
                zero = jnp.zeros_like(v)
                stacked = jnp.concatenate([pair(v, zero), pair(zero, v)], axis=0)
                y_buf[:, cols] = jnp.dot(
                    jnp.concatenate(weights, axis=1), stacked, preferred_element_type=F32
                )
                tail = pair(tails[:, h : h + 1], tails[:, h + 1 : h + 2])
                scaled = (v.astype(F32) * tail).astype(BF16)
                update = lax.dot_general(
                    b, scaled, (((0,), (0,)), ((), ())), preferred_element_type=F32
                ).astype(BF16)
                dec = jnp.where(left_row, total[:, h : h + 1], total[:, h + 1 : h + 2])
                high = dec.astype(BF16).astype(F32)
                mid = (dec - high).astype(BF16).astype(F32)
                low = dec - high - mid
                extra = jnp.where(
                    extra_row == 0, high, jnp.where(extra_row == 1, mid, low)
                ).astype(BF16)
                k = gi * 4 + hp
                if width >= 128:
                    per = width // 128
                    to = gp * (8 // per) + k // per
                    at = (k % per) * 128
                    st_send[to, :N, at : at + 128] = update
                    st_send[to, N:, at : at + 128] = extra
                else:
                    per = 128 // width
                    for part in range(per):
                        to = gp * 8 * per + k * per + part
                        lanes = slice(part * width, (part + 1) * width)
                        st_send[to, :N, :] = update[:, lanes]
                        st_send[to, N:, :] = extra[:, lanes]

        @pl.loop(0, per_gp)
        def _(i):
            to = gp * per_gp + i

            @pl.when(to != me)
            def _():
                st_copy(to).start()

            @pl.when(to == me)
            def _():
                st_recv[me] = st_send[me]

    down.step(0)

    def back_copy(to):
        return remote(st_back.at[to], st_enter.at[me], back_sem.at[to], back_rsem.at[me], to)

    def advance(i, state):
        @pl.when(i != me)
        def _():
            remote(
                st_send.at[i], st_recv.at[i], st_sem.at[i], st_rsem.at[i], i
            ).wait_recv()

        block = st_recv[i].astype(F32)
        dec = block[N : N + 1] + block[N + 1 : N + 2] + block[N + 2 : N + 3]
        st_back[i] = state.astype(BF16)

        @pl.when(i != me)
        def _():
            back_copy(i).start()

        @pl.when(i == me)
        def _():
            st_enter[me] = st_back[me]

        return dec * state + block[:N]

    lax.fori_loop(0, n, advance, jnp.zeros((N, width), F32))
    if half > 1:
        down.step(1)

    @pl.loop(1, n)
    def _(i):
        src = lax.rem(me + i, n)
        remote(
            st_back.at[src], st_enter.at[src], back_sem.at[src], back_rsem.at[src], src
        ).wait_recv()

    def finish_mixer(gp, squares):
        reach_scale = jnp.exp(logs_t[gp])
        c2 = out_c[:, pl.ds(pl.multiple_of(gp * 128, 128), 128)]
        for gi in range(2):
            c = c2[:, gi * N : (gi + 1) * N]
            for hp in range(4):
                h = gi * 8 + hp * 2
                cols = pl.ds(pl.multiple_of(gp * 1024 + gi * 512 + hp * 128, 128), 128)
                k = gi * 4 + hp
                if width >= 128:
                    per = width // 128
                    at = (k % per) * 128
                    enter = st_enter[gp * (8 // per) + k // per, :, at : at + 128]
                else:
                    per = 128 // width
                    first = gp * 8 * per + k * per
                    enter = jnp.concatenate([st_enter[first + j] for j in range(per)], axis=1)
                reach = jnp.dot(c, enter, preferred_element_type=F32)
                y = y_buf[:, cols] + pair(reach_scale[:, h : h + 1], reach_scale[:, h + 1 : h + 2]) * reach
                square = y * y
                both = jnp.sum(square, axis=1, keepdims=True)
                one = jnp.sum(jnp.where(left, square, 0.0), axis=1, keepdims=True)
                other = jnp.sum(jnp.where(left, 0.0, square), axis=1, keepdims=True)
                del both
                scale = pair(
                    lax.rsqrt(one * (1.0 / P_SIZE) + 1e-05),
                    lax.rsqrt(other * (1.0 / P_SIZE) + 1e-05),
                )
                mixed = (
                    residual[:, cols].astype(F32) + y * scale * mixer_gain[:, cols]
                ).astype(BF16)
                mixed_out[:, cols] = mixed
                wide = mixed.astype(F32)
                squares = squares + wide * wide
        return squares

    squares = lax.fori_loop(0, 4, finish_mixer, jnp.zeros((tok, 128), F32))
    mean = jnp.sum(squares, axis=1, keepdims=True) * (1.0 / (n * width))
    row_scale = lax.rsqrt(mean + 1e-05)
    rows = w_buf.shape[1]
    if rows >= 128:

        @pl.loop(0, n)
        def _(i):
            cols = pl.ds(pl.multiple_of(i * rows, rows), rows)
            wide = mixed_out[:, cols].astype(F32)
            normed[i] = (wide * row_scale * moe_gain[:, cols]).astype(BF16)
    else:

        @pl.loop(0, n // 2)
        def _(i):
            cols = pl.ds(pl.multiple_of(i * 128, 128), 128)
            wide = mixed_out[:, cols].astype(F32)
            both = (wide * row_scale * moe_gain[:, cols]).astype(BF16)
            normed[2 * i] = both[:, :rows]
            normed[2 * i + 1] = both[:, rows:]

    for step in range(2, half):
        down.step(step)
    for step in range(-1, half):
        down.wait_side(step)
    acc[...] = jnp.zeros_like(acc)

    @pl.loop(0, n)
    def _(i):
        acc[...] += jnp.dot(normed[i], w_buf[i], preferred_element_type=F32)

    lat_buf[me] = acc[...].astype(BF16)

    lat = Gather(lat_buf, chips, place, core, (l_ring_s, l_ring_r, l_side_s, l_side_r))
    lat.start()

    @pl.loop(1, n)
    def _(i):
        src = lax.rem(me + i, n)
        remote(
            gates.at[src], gate_buf.at[src], gate_sem.at[src], gate_rsem.at[src], src
        ).wait_recv()

    load_in.wait()
    load_out.wait()

    def expert(place_of):
        chip = ring_chip(chips, place_of)
        x = lat_buf[pl.ds(2 * chip, 2)].reshape(2 * tok, lat_buf.shape[2])
        hidden = jnp.dot(x, win_buf[...], preferred_element_type=F32)
        hidden = jnp.square(jnp.maximum(hidden, 0.0)).astype(BF16)
        out = jnp.dot(hidden, wout_buf[...], preferred_element_type=F32).astype(BF16).astype(F32)
        for k in range(2):
            gate = jnp.transpose(gate_buf[2 * chip + k])[:, :1]
            parts[2 * chip + k] = (out[k * tok : (k + 1) * tok] * gate).astype(BF16)

    def part_copy(index, place_of):
        chip = ring_chip(chips, place_of)
        return remote(
            parts.at[2 * chip + 1 - core],
            side_parts.at[chip],
            p_side_s.at[index],
            p_side_r.at[index],
            ring_chip(chips, place) * 2 + 1 - core,
        )

    def work(step):
        if step < 0:
            expert(place)
            part_copy(0, place).start()
        elif step == half - 1:
            expert(place + half)
            part_copy(2 * half - 1, place + half).start()
        else:

            @pl.loop(0, 2)
            def _(way):
                there = place - (1 - 2 * way) * (step + 1)
                expert(there)
                part_copy(1 + 2 * step + way, there).start()

    if apart:
        for step in range(half):
            lat.step(step)
            lat.wait_side(step - 1)
            work(step - 1)
        lat.wait_side(half - 1)
        work(half - 1)
        lat.finish()
    else:
        for step in range(half):
            lat.step(step)
        for step in range(-1, half):
            lat.wait_side(step)
        lat.finish()
        for step in range(-1, half):
            work(step)

    def pair_sum(index, place_of):
        chip = ring_chip(chips, place_of)
        part_copy(index, place_of).wait_recv()
        slot = 2 * chip + core
        parts[slot] = (parts[slot].astype(F32) + side_parts[chip].astype(F32)).astype(BF16)

    cut = tok // 2

    def sum_copy(way, step):
        sign = 1 - 2 * way
        there = place + sign * (half - step)
        block = parts.at[2 * ring_chip(chips, there) + core]
        to = ring_chip(chips, place + sign) * 2 + core
        if step == 0:
            block = block.at[pl.ds(way * cut, cut)]
            target = half_sums.at[way]
        else:
            target = sums.at[way * (half - 1) + step - 1]
        sem = way * half + step
        return remote(block, target, s_send.at[sem], s_recv.at[sem], to)

    sent = []
    pair_sum(2 * half - 1, place + half)
    for way in range(2):
        sent.append(sum_copy(way, 0))
        sent[-1].start()
    for step in range(1, half):
        for way in range(2):
            there = place + (1 - 2 * way) * (half - step)
            pair_sum(1 + 2 * (half - step - 1) + (1 - way), there)
        for way in range(2):
            there = place + (1 - 2 * way) * (half - step)
            slot = 2 * ring_chip(chips, there) + core
            sum_copy(way, step - 1).wait_recv()
            if step == 1:
                some = pl.ds(way * cut, cut)
                parts[slot, some] = (
                    parts[slot, some].astype(F32) + half_sums[way].astype(F32)
                ).astype(BF16)
            else:
                parts[slot] = (
                    parts[slot].astype(F32)
                    + sums[way * (half - 1) + step - 2].astype(F32)
                ).astype(BF16)
            sent.append(sum_copy(way, step))
            sent[-1].start()
    part_copy(0, place).wait_recv()
    mine = ring_chip(chips, place)
    whole = parts[2 * mine + core].astype(F32) + side_parts[mine].astype(F32)
    for way in range(2):
        sum_copy(way, half - 1).wait_recv()
        whole = whole + sums[way * (half - 1) + half - 2].astype(F32)
    mix_out[...] = whole.astype(BF16)

    for copy in sent:
        copy.wait_send()
    for index in range(2 * half):
        part_copy(index, place).wait_send()
    down.finish()

    @pl.loop(1, n)
    def _(i):
        to = lax.rem(me + i, n)
        st_copy(to).wait_send()
        back_copy(to).wait_send()
        gate_copy(to).wait_send()


def on_device(
    values,
    in_b,
    out_c,
    decay_log,
    residual,
    mixer_gain,
    moe_gain,
    w_down,
    w_in,
    w_out,
    routes,
    gate_int,
):
    n = lax.axis_size("ctx")
    tok, width = values.shape
    latent = w_down.shape[1]
    chips = n // 2
    half = chips // 2
    gate_float = gate_int.astype(F32)
    gate = gate_float / jnp.sum(gate_float, axis=1, keepdims=True)
    named = routes[None] == jnp.arange(n, dtype=jnp.int32)[:, None, None]
    table = jnp.sum(jnp.where(named, gate[None], 0.0), axis=2)
    gates = jnp.broadcast_to(table[:, None, :], (n, 8, tok))
    vmem = pl.BlockSpec(memory_space=pltpu.VMEM)
    anywhere = pl.BlockSpec(memory_space=pl.ANY)
    dma = lambda count: pltpu.SemaphoreType.DMA((count,))
    share = width // n
    scratch = [
        pltpu.VMEM((n,) + w_down.shape, BF16),
        pltpu.VMEM((n, tok, latent), BF16),
    ]
    if n <= 16:
        scratch.append(pltpu.VMEM((n, tok, latent), BF16))
    scratch += [
        pltpu.VMEM((tok, width), F32),
        pltpu.VMEM((4, tok, 16), F32),
        pltpu.VMEM((n, tok, w_down.shape[0]), BF16),
        pltpu.VMEM((tok, latent), F32),
        pltpu.VMEM((n, N + EXTRA, share), BF16),
        pltpu.VMEM((n, N + EXTRA, share), BF16),
        pltpu.VMEM((n, N, share), BF16),
        pltpu.VMEM((n, N, share), BF16),
        pltpu.VMEM((n, 8, tok), F32),
        pltpu.VMEM(w_in.shape[1:], BF16),
        pltpu.VMEM(w_out.shape[1:], BF16),
        pltpu.VMEM((chips, tok, latent), BF16),
        pltpu.VMEM((2 * (half - 1), tok, latent), BF16),
        pltpu.VMEM((2, tok // 2, latent), BF16),
        dma(3),
    ]
    scratch += [dma(n)] * 6
    scratch += [dma(2 * half), dma(2 * half), dma(2 * half + 1), dma(2 * half + 1)] * 2
    scratch += [dma(2 * half)] * 4
    return pl.pallas_call(
        functools.partial(kernel, n),
        out_shape=(
            jax.ShapeDtypeStruct((tok, width), BF16),
            jax.ShapeDtypeStruct((tok, latent), BF16),
        ),
        in_specs=[vmem] * 8 + [anywhere] * 3,
        out_specs=(vmem, vmem),
        scratch_shapes=scratch,
        compiler_params=pltpu.CompilerParams(
            collective_id=0, has_side_effects=True, vmem_limit_bytes=62 * 1024 * 1024
        ),
    )(
        values,
        in_b,
        out_c,
        decay_log,
        residual,
        mixer_gain.reshape(1, -1),
        moe_gain.reshape(1, -1),
        gates,
        w_down,
        w_in,
        w_out,
    )


def solution(mesh):
    return jax.shard_map(
        on_device,
        mesh=mesh,
        in_specs=(
            P(("groups", "ctx"), None),
            P(("groups", "ctx"), None),
            P(("groups", "ctx"), None),
            P(None, ("groups", "ctx")),
            P(("groups", "ctx"), None),
            P(),
            P(),
            P("ctx", None),
            P("ctx", None, None),
            P("ctx", None, None),
            P(("groups", "ctx"), None),
            P(("groups", "ctx"), None),
        ),
        out_specs=(P(("groups", "ctx"), None), P(("groups", "ctx"), None)),
        check_vma=False,
    )
```

```python
import functools

import jax
import jax.numpy as jnp
from jax import lax
from jax.experimental import pallas as pl
from jax.experimental.pallas import tpu as pltpu
from jax.sharding import PartitionSpec as P

P_SIZE = 64
N = 64
GROUPS = 8
EXTRA = 16
MESH = pl.DeviceIdType.MESH
F32 = jnp.float32
BF16 = jnp.bfloat16


def ring_place(chips, chip):
    if chips == 8:
        z, y = chip // 2, chip % 2
        return z * (1 - y) + (7 - z) * y
    return chip


def ring_chip(chips, place):
    place = lax.rem(place + 2 * chips, chips)
    if chips == 8:
        back = place // 4
        return (1 - back) * (2 * place) + back * (2 * (7 - place) + 1)
    return place


def remote(src, dst, send, recv, device):
    return pltpu.make_async_remote_copy(
        src_ref=src,
        dst_ref=dst,
        send_sem=send,
        recv_sem=recv,
        device_id={"ctx": device},
        device_id_type=MESH,
    )


class Gather:
    def __init__(self, buf, chips, place, core, sems, skip=0, parity=0, partner=0):
        self.buf, self.chips, self.place, self.core = buf, chips, place, core
        self.half = chips // 2
        self.rows = buf.shape[1]
        self.skip, self.parity, self.partner = skip, parity, partner
        self.piece = (self.rows - skip) // 2
        self.ring_send, self.ring_recv, self.side_send, self.side_recv = sems[:4]
        self.cross = sems[4:]
        self.started = []

    def slot(self, place, core=None):
        return ring_chip(self.chips, place) * 2 + (self.core if core is None else core)

    def rows_at(self, place, start, count, core=None):
        return self.buf.at[self.slot(place, core), pl.ds(pl.multiple_of(start, 16), count)]

    def part(self, place, piece, core=None):
        return self.rows_at(place, self.parity * self.skip + piece * self.piece, self.piece, core)

    def pieces(self, way, step):
        return (way,) if step == self.half - 1 else (way, 1 - way)

    def index(self, way, step, piece):
        return (way * self.half + step) * 2 + piece

    def ring(self, way, step, piece):
        sign = 1 - 2 * way
        block = self.part(self.place - sign * (step + 1), piece)
        sem = self.index(way, step, piece)
        return remote(
            block, block, self.ring_send.at[sem], self.ring_recv.at[sem], self.slot(self.place + sign)
        )

    def side(self, index, block):
        return remote(
            block,
            block,
            self.side_send.at[index],
            self.side_recv.at[index],
            self.slot(self.place, 1 - self.core),
        )

    def go(self, copy):
        copy.start()
        self.started.append(copy)

    def send(self, way, step, piece):
        sign = 1 - 2 * way
        block = self.part(self.place - sign * step, piece)
        sem = self.index(way, step, piece)
        self.go(
            remote(
                block,
                block,
                self.ring_send.at[sem],
                self.ring_recv.at[sem],
                self.slot(self.place + sign),
            )
        )

    def start(self):
        for k in range(2):
            for way in range(2):
                self.send(way, 0, self.pieces(way, 0)[k])
        self.go(self.side(0, self.buf.at[self.slot(self.place)]))

    def far(self, step):
        if step == self.half - 1:
            return ((2 * step, self.place + self.half),)
        return tuple((2 * step + way, self.place - (1 - 2 * way) * (step + 1)) for way in range(2))

    def crossing(self, index, place, mine, core=None):
        start = (self.parity if mine else 1 - self.parity) * (self.rows - self.skip)
        block = self.rows_at(place, start, self.skip, core)
        if core is None:
            return pltpu.make_async_remote_copy(
                src_ref=block,
                dst_ref=block,
                send_sem=self.cross[0].at[index],
                recv_sem=self.cross[1].at[index],
                device_id={"groups": self.partner},
                device_id_type=MESH,
            )
        return remote(
            block,
            block,
            self.cross[2].at[index],
            self.cross[3].at[index],
            self.slot(self.place, 1 - self.core),
        )

    def step(self, step):
        for k in range(len(self.pieces(0, step))):
            for way in range(2):
                piece = self.pieces(way, step)[k]
                self.ring(way, step, piece).wait_recv()
                if step + 1 < self.half and piece in self.pieces(way, step + 1):
                    self.send(way, step + 1, piece)
                sign = 1 - 2 * way
                came = self.part(self.place - sign * (step + 1), piece)
                self.go(self.side(1 + self.index(way, step, piece), came))
        if self.skip:
            for index, place in self.far(step):
                self.go(self.crossing(index, place, True))
            if step:
                self.cross_step(step - 1)

    def cross_step(self, step):
        for index, place in self.far(step):
            self.crossing(index, place, False).wait_recv()
            self.go(self.crossing(index, place, False, self.core))

    def wait_side(self, step):
        other = 1 - self.core
        if step < 0:
            self.side(0, self.buf.at[self.slot(self.place, other)]).wait_recv()
            return
        for way in range(2):
            for piece in self.pieces(way, step):
                block = self.part(self.place - (1 - 2 * way) * (step + 1), piece, other)
                self.side(1 + self.index(way, step, piece), block).wait_recv()
        if self.skip:
            for index, place in self.far(step):
                self.crossing(index, place, False, other).wait_recv()

    def finish(self):
        for copy in self.started:
            copy.wait_send()
        self.started = []


def kernel(
    n,
    skip,
    values,
    in_b,
    out_c,
    decay_log,
    residual,
    mixer_gain,
    moe_gain,
    gates,
    w_down,
    w_in,
    w_out,
    mixed_out,
    mix_out,
    w_buf,
    lat_buf,
    *rest,
):
    chips = n // 2
    half = chips // 2
    apart = n <= 16
    if apart:
        parts, rest = rest[0], rest[1:]
    else:
        parts = lat_buf
    (
        y_buf,
        logs_t,
        normed,
        acc,
        st_send,
        st_recv,
        st_back,
        st_enter,
        before,
        tot_send,
        tot_recv,
        carry,
        gate_buf,
        win_buf,
        wout_buf,
        side_parts,
        sums,
        half_sums,
        local_sem,
        st_sem,
        st_rsem,
        back_sem,
        back_rsem,
        tot_sem,
        tot_rsem,
        gate_sem,
        gate_rsem,
        w_ring_s,
        w_ring_r,
        w_side_s,
        w_side_r,
        x_send,
        x_recv,
        x_side_s,
        x_side_r,
        l_ring_s,
        l_ring_r,
        l_side_s,
        l_side_r,
        p_side_s,
        p_side_r,
        s_send,
        s_recv,
    ) = rest
    me = lax.axis_index("ctx")
    core = lax.rem(me, 2)
    place = ring_place(chips, me // 2)
    tok = values.shape[0]
    width = values.shape[1] // n

    load_down = pltpu.make_async_copy(w_down, w_buf.at[me], local_sem.at[0])
    load_in = pltpu.make_async_copy(w_in.at[0], win_buf, local_sem.at[1])
    load_out = pltpu.make_async_copy(w_out.at[0], wout_buf, local_sem.at[2])
    load_down.start()
    load_in.start()
    load_out.start()

    barrier = pltpu.get_barrier_semaphore()

    @pl.loop(1, n)
    def _(i):
        pl.semaphore_signal(
            barrier, inc=1, device_id={"ctx": lax.rem(me + i, n)}, device_id_type=MESH
        )

    group = lax.axis_index("groups")
    parity = lax.rem(group, 2)
    partner = group + 1 - 2 * parity
    if skip:
        pl.semaphore_signal(
            barrier, inc=1, device_id={"groups": partner}, device_id_type=MESH
        )
    pl.semaphore_wait(barrier, n if skip else n - 1)
    load_down.wait()
    down = Gather(
        w_buf,
        chips,
        place,
        core,
        (w_ring_s, w_ring_r, w_side_s, w_side_r, x_send, x_recv, x_side_s, x_side_r),
        skip,
        parity,
        partner,
    )
    down.start()

    def gate_copy(to):
        return remote(gates.at[to], gate_buf.at[me], gate_sem.at[to], gate_rsem.at[me], to)

    @pl.loop(1, n)
    def _(i):
        gate_copy(lax.rem(me + i, n)).start()

    gate_buf[me] = gates[me]

    row = lax.broadcasted_iota(jnp.int32, (tok, tok), 0)
    col = lax.broadcasted_iota(jnp.int32, (tok, tok), 1)
    lower = row >= col
    lower_f = lower.astype(F32)
    upper_f = (row <= col).astype(F32)
    left = lax.broadcasted_iota(jnp.int32, (tok, 128), 1) < P_SIZE
    left_row = left[:1]
    extra_row = lax.broadcasted_iota(jnp.int32, (EXTRA, 128), 0)

    def pair(a, b):
        return jnp.where(left, a, b)

    plane, quarter = me // 4, lax.rem(me, 4)
    planes = n // 4

    def st_copy(to):
        return remote(
            st_send.at[to], st_recv.at[quarter], st_sem.at[to], st_rsem.at[quarter], plane * 4 + to
        )

    @pl.loop(0, 4)
    def _(gp):
        logs = decay_log[pl.ds(pl.multiple_of(gp * 16, 16), 16), :]
        run = jnp.dot(logs, upper_f, precision=lax.Precision.HIGHEST, preferred_element_type=F32)
        run_t = lax.dot_general(
            lower_f,
            logs,
            (((1,), (1,)), ((), ())),
            precision=lax.Precision.HIGHEST,
            preferred_element_type=F32,
        )
        logs_t[gp] = run_t
        tails = jnp.exp(run_t[tok - 1 : tok, :] - run_t)
        total = jnp.exp(run_t[tok - 1 : tok, :])
        two = pl.ds(pl.multiple_of(gp * 128, 128), 128)
        b2, c2 = in_b[:, two], out_c[:, two]
        for gi in range(2):
            b = b2[:, gi * N : (gi + 1) * N]
            c = c2[:, gi * N : (gi + 1) * N]
            scores = lax.dot_general(c, b, (((1,), (1,)), ((), ())), preferred_element_type=F32)
            for hp in range(4):
                h = gi * 8 + hp * 2
                cols = pl.ds(pl.multiple_of(gp * 1024 + gi * 512 + hp * 128, 128), 128)
                v = values[:, cols]
                weights = []
                for k in range(2):
                    spread = run_t[:, h + k : h + k + 1] - run[h + k : h + k + 1, :]
                    decays = jnp.exp(jnp.where(lower, spread, -1e30))
                    weights.append((scores * decays).astype(BF16))
                zero = jnp.zeros_like(v)
                stacked = jnp.concatenate([pair(v, zero), pair(zero, v)], axis=0)
                y_buf[:, cols] = jnp.dot(
                    jnp.concatenate(weights, axis=1), stacked, preferred_element_type=F32
                )
                tail = pair(tails[:, h : h + 1], tails[:, h + 1 : h + 2])
                scaled = (v.astype(F32) * tail).astype(BF16)
                update = lax.dot_general(
                    b, scaled, (((0,), (0,)), ((), ())), preferred_element_type=F32
                ).astype(BF16)
                dec = jnp.where(left_row, total[:, h : h + 1], total[:, h + 1 : h + 2])
                high = dec.astype(BF16).astype(F32)
                mid = (dec - high).astype(BF16).astype(F32)
                low = dec - high - mid
                extra = jnp.where(
                    extra_row == 0, high, jnp.where(extra_row == 1, mid, low)
                ).astype(BF16)
                at = gi * 512 + hp * 128
                st_send[gp, :N, at : at + 128] = update
                st_send[gp, N:, at : at + 128] = extra

        @pl.when(gp != quarter)
        def _():
            st_copy(gp).start()

        @pl.when(gp == quarter)
        def _():
            st_recv[quarter] = st_send[quarter]

    def take(block):
        block = block.astype(F32)
        return block[N : N + 1] + block[N + 1 : N + 2] + block[N + 2 : N + 3], block[:N]

    state = jnp.zeros((N, 1024), F32)
    total = jnp.ones((1, 1024), F32)
    for i in range(4):

        @pl.when(quarter != i)
        def _():
            remote(
                st_send.at[i], st_recv.at[i], st_sem.at[i], st_rsem.at[i], plane * 4 + i
            ).wait_recv()

        before[i, :N] = state
        before[i, N : N + 8] = jnp.broadcast_to(total, (8, 1024))
        dec, update = take(st_recv[i])
        state = dec * state + update
        total = dec * total
    high = total.astype(BF16).astype(F32)
    mid = (total - high).astype(BF16).astype(F32)
    place_row = lax.broadcasted_iota(jnp.int32, (EXTRA, 1024), 0)
    tot_send[:N] = state.astype(BF16)
    tot_send[N:] = jnp.where(
        place_row == 0, high, jnp.where(place_row == 1, mid, total - high - mid)
    ).astype(BF16)

    def tot_copy(to):
        return remote(
            tot_send, tot_recv.at[plane], tot_sem.at[to], tot_rsem.at[plane], to * 4 + quarter
        )

    @pl.loop(0, planes)
    def _(to):
        @pl.when(to > plane)
        def _():
            tot_copy(to).start()

    down.step(0)
    carry[...] = jnp.zeros_like(carry)

    @pl.loop(0, planes)
    def _(i):
        @pl.when(i < plane)
        def _():
            remote(
                tot_send, tot_recv.at[i], tot_sem.at[i], tot_rsem.at[i], i * 4 + quarter
            ).wait_recv()
            dec, update = take(tot_recv[i])
            carry[...] = dec * carry[...] + update

    def back_copy(to):
        return remote(
            st_back.at[to], st_enter.at[quarter], back_sem.at[to], back_rsem.at[quarter], plane * 4 + to
        )

    for i in range(4):
        st_back[i] = (before[i, :N] + before[i, N : N + 1] * carry[...]).astype(BF16)

        @pl.when(quarter != i)
        def _():
            back_copy(i).start()

        @pl.when(quarter == i)
        def _():
            st_enter[quarter] = st_back[quarter]

    for step in range(1, half - 1):
        down.step(step)

    @pl.loop(1, 4)
    def _(i):
        src = lax.rem(quarter + i, 4)
        remote(
            st_back.at[src],
            st_enter.at[src],
            back_sem.at[src],
            back_rsem.at[src],
            plane * 4 + src,
        ).wait_recv()

    def finish_mixer(gp, squares):
        reach_scale = jnp.exp(logs_t[gp])
        c2 = out_c[:, pl.ds(pl.multiple_of(gp * 128, 128), 128)]
        for gi in range(2):
            c = c2[:, gi * N : (gi + 1) * N]
            for hp in range(4):
                h = gi * 8 + hp * 2
                cols = pl.ds(pl.multiple_of(gp * 1024 + gi * 512 + hp * 128, 128), 128)
                at = gi * 512 + hp * 128
                enter = st_enter[gp, :, at : at + 128]
                reach = jnp.dot(c, enter, preferred_element_type=F32)
                y = y_buf[:, cols] + pair(reach_scale[:, h : h + 1], reach_scale[:, h + 1 : h + 2]) * reach
                square = y * y
                both = jnp.sum(square, axis=1, keepdims=True)
                one = jnp.sum(jnp.where(left, square, 0.0), axis=1, keepdims=True)
                other = jnp.sum(jnp.where(left, 0.0, square), axis=1, keepdims=True)
                del both
                scale = pair(
                    lax.rsqrt(one * (1.0 / P_SIZE) + 1e-05),
                    lax.rsqrt(other * (1.0 / P_SIZE) + 1e-05),
                )
                mixed = (
                    residual[:, cols].astype(F32) + y * scale * mixer_gain[:, cols]
                ).astype(BF16)
                mixed_out[:, cols] = mixed
                wide = mixed.astype(F32)
                squares = squares + wide * wide
        return squares

    squares = lax.fori_loop(0, 4, finish_mixer, jnp.zeros((tok, 128), F32))
    mean = jnp.sum(squares, axis=1, keepdims=True) * (1.0 / (n * width))
    row_scale = lax.rsqrt(mean + 1e-05)
    rows = w_buf.shape[1]
    if rows >= 128:

        @pl.loop(0, n)
        def _(i):
            cols = pl.ds(pl.multiple_of(i * rows, rows), rows)
            wide = mixed_out[:, cols].astype(F32)
            normed[i] = (wide * row_scale * moe_gain[:, cols]).astype(BF16)
    else:

        @pl.loop(0, n // 2)
        def _(i):
            cols = pl.ds(pl.multiple_of(i * 128, 128), 128)
            wide = mixed_out[:, cols].astype(F32)
            both = (wide * row_scale * moe_gain[:, cols]).astype(BF16)
            normed[2 * i] = both[:, :rows]
            normed[2 * i + 1] = both[:, rows:]

    for step in range(half - 1, half):
        down.step(step)
    if skip:
        down.cross_step(half - 1)
    for step in range(-1, half):
        down.wait_side(step)
    acc[...] = jnp.zeros_like(acc)

    @pl.loop(0, n)
    def _(i):
        acc[...] += jnp.dot(normed[i], w_buf[i], preferred_element_type=F32)

    lat_buf[me] = acc[...].astype(BF16)

    lat = Gather(lat_buf, chips, place, core, (l_ring_s, l_ring_r, l_side_s, l_side_r))
    lat.start()

    @pl.loop(1, n)
    def _(i):
        src = lax.rem(me + i, n)
        remote(
            gates.at[src], gate_buf.at[src], gate_sem.at[src], gate_rsem.at[src], src
        ).wait_recv()

    load_in.wait()
    load_out.wait()

    def expert(place_of):
        chip = ring_chip(chips, place_of)
        x = lat_buf[pl.ds(2 * chip, 2)].reshape(2 * tok, lat_buf.shape[2])
        hidden = jnp.dot(x, win_buf[...], preferred_element_type=F32)
        hidden = jnp.square(jnp.maximum(hidden, 0.0)).astype(BF16)
        out = jnp.dot(hidden, wout_buf[...], preferred_element_type=F32).astype(BF16).astype(F32)
        for k in range(2):
            gate = jnp.transpose(gate_buf[2 * chip + k])[:, :1]
            parts[2 * chip + k] = (out[k * tok : (k + 1) * tok] * gate).astype(BF16)

    def part_copy(index, place_of):
        chip = ring_chip(chips, place_of)
        return remote(
            parts.at[2 * chip + 1 - core],
            side_parts.at[chip],
            p_side_s.at[index],
            p_side_r.at[index],
            ring_chip(chips, place) * 2 + 1 - core,
        )

    def work(step):
        if step < 0:
            expert(place)
            part_copy(0, place).start()
        elif step == half - 1:
            expert(place + half)
            part_copy(2 * half - 1, place + half).start()
        else:

            @pl.loop(0, 2)
            def _(way):
                there = place - (1 - 2 * way) * (step + 1)
                expert(there)
                part_copy(1 + 2 * step + way, there).start()

    if apart:
        for step in range(half):
            lat.step(step)
            lat.wait_side(step - 1)
            work(step - 1)
        lat.wait_side(half - 1)
        work(half - 1)
        lat.finish()
    else:
        for step in range(half):
            lat.step(step)
        for step in range(-1, half):
            lat.wait_side(step)
        lat.finish()
        for step in range(-1, half):
            work(step)

    def pair_sum(index, place_of):
        chip = ring_chip(chips, place_of)
        part_copy(index, place_of).wait_recv()
        slot = 2 * chip + core
        parts[slot] = (parts[slot].astype(F32) + side_parts[chip].astype(F32)).astype(BF16)

    cut = tok // 2

    def sum_copy(way, step, piece):
        sign = 1 - 2 * way
        there = place + sign * (half - step)
        some = pl.ds(piece * cut, cut)
        block = parts.at[2 * ring_chip(chips, there) + core, some]
        to = ring_chip(chips, place + sign) * 2 + core
        if step == 0:
            target = half_sums.at[way]
        else:
            target = sums.at[way * (half - 1) + step - 1, some]
        sem = (way * half + step) * 2 + piece
        return remote(block, target, s_send.at[sem], s_recv.at[sem], to)

    sent = []

    def send_sum(way, step, piece):
        sent.append(sum_copy(way, step, piece))
        sent[-1].start()

    pair_sum(2 * half - 1, place + half)
    for way in range(2):
        send_sum(way, 0, way)
    for step in range(1, half):
        for way in range(2):
            there = place + (1 - 2 * way) * (half - step)
            pair_sum(1 + 2 * (half - step - 1) + (1 - way), there)
        for first in (True, False):
            for way in range(2):
                piece = 1 - way if first else way
                there = place + (1 - 2 * way) * (half - step)
                slot = 2 * ring_chip(chips, there) + core
                some = pl.ds(piece * cut, cut)
                if step > 1 or not first:
                    sum_copy(way, step - 1, piece).wait_recv()
                    if step == 1:
                        came = half_sums[way]
                    else:
                        came = sums[way * (half - 1) + step - 2, some]
                    parts[slot, some] = (
                        parts[slot, some].astype(F32) + came.astype(F32)
                    ).astype(BF16)
                send_sum(way, step, piece)
    part_copy(0, place).wait_recv()
    mine = ring_chip(chips, place)
    whole = parts[2 * mine + core].astype(F32) + side_parts[mine].astype(F32)
    for way in range(2):
        for piece in range(2):
            sum_copy(way, half - 1, piece).wait_recv()
        whole = whole + sums[way * (half - 1) + half - 2].astype(F32)
    mix_out[...] = whole.astype(BF16)

    for copy in sent:
        copy.wait_send()
    for index in range(2 * half):
        part_copy(index, place).wait_send()
    down.finish()

    @pl.loop(1, n)
    def _(i):
        to = lax.rem(me + i, n)
        gate_copy(to).wait_send()

    @pl.loop(1, 4)
    def _(i):
        to = lax.rem(quarter + i, 4)
        st_copy(to).wait_send()
        back_copy(to).wait_send()

    @pl.loop(0, planes)
    def _(to):
        @pl.when(to > plane)
        def _():
            tot_copy(to).wait_send()


def on_device(
    values,
    in_b,
    out_c,
    decay_log,
    residual,
    mixer_gain,
    moe_gain,
    w_down,
    w_in,
    w_out,
    routes,
    gate_int,
):
    n = lax.axis_size("ctx")
    tok, width = values.shape
    latent = w_down.shape[1]
    chips = n // 2
    half = chips // 2
    gate_float = gate_int.astype(F32)
    gate = gate_float / jnp.sum(gate_float, axis=1, keepdims=True)
    named = routes[None] == jnp.arange(n, dtype=jnp.int32)[:, None, None]
    table = jnp.sum(jnp.where(named, gate[None], 0.0), axis=2)
    gates = jnp.broadcast_to(table[:, None, :], (n, 8, tok))
    vmem = pl.BlockSpec(memory_space=pltpu.VMEM)
    anywhere = pl.BlockSpec(memory_space=pl.ANY)
    dma = lambda count: pltpu.SemaphoreType.DMA((count,))
    scratch = [
        pltpu.VMEM((n,) + w_down.shape, BF16),
        pltpu.VMEM((n, tok, latent), BF16),
    ]
    if n <= 16:
        scratch.append(pltpu.VMEM((n, tok, latent), BF16))
    scratch += [
        pltpu.VMEM((tok, width), F32),
        pltpu.VMEM((4, tok, 16), F32),
        pltpu.VMEM((n, tok, w_down.shape[0]), BF16),
        pltpu.VMEM((tok, latent), F32),
        pltpu.VMEM((4, N + EXTRA, 1024), BF16),
        pltpu.VMEM((4, N + EXTRA, 1024), BF16),
        pltpu.VMEM((4, N, 1024), BF16),
        pltpu.VMEM((4, N, 1024), BF16),
        pltpu.VMEM((4, N + 8, 1024), F32),
        pltpu.VMEM((N + EXTRA, 1024), BF16),
        pltpu.VMEM((n // 4, N + EXTRA, 1024), BF16),
        pltpu.VMEM((N, 1024), F32),
        pltpu.VMEM((n, 8, tok), F32),
        pltpu.VMEM(w_in.shape[1:], BF16),
        pltpu.VMEM(w_out.shape[1:], BF16),
        pltpu.VMEM((chips, tok, latent), BF16),
        pltpu.VMEM((2 * (half - 1), tok, latent), BF16),
        pltpu.VMEM((2, tok // 2, latent), BF16),
        dma(3),
    ]
    scratch += [dma(4)] * 4 + [dma(n // 4)] * 2 + [dma(n)] * 2
    ring = [dma(4 * half)] * 2 + [dma(4 * half + 1)] * 2
    scratch += ring + [dma(2 * half)] * 4 + ring
    scratch += [dma(2 * half)] * 2 + [dma(4 * half)] * 2
    skip = w_down.shape[0] // 4 // 32 * 32 if lax.axis_size("groups") % 2 == 0 else 0
    return pl.pallas_call(
        functools.partial(kernel, n, skip),
        out_shape=(
            jax.ShapeDtypeStruct((tok, width), BF16),
            jax.ShapeDtypeStruct((tok, latent), BF16),
        ),
        in_specs=[vmem] * 8 + [anywhere] * 3,
        out_specs=(vmem, vmem),
        scratch_shapes=scratch,
        compiler_params=pltpu.CompilerParams(
            collective_id=0, has_side_effects=True, vmem_limit_bytes=62 * 1024 * 1024
        ),
    )(
        values,
        in_b,
        out_c,
        decay_log,
        residual,
        mixer_gain.reshape(1, -1),
        moe_gain.reshape(1, -1),
        gates,
        w_down,
        w_in,
        w_out,
    )


def solution(mesh):
    return jax.shard_map(
        on_device,
        mesh=mesh,
        in_specs=(
            P(("groups", "ctx"), None),
            P(("groups", "ctx"), None),
            P(("groups", "ctx"), None),
            P(None, ("groups", "ctx")),
            P(("groups", "ctx"), None),
            P(),
            P(),
            P("ctx", None),
            P("ctx", None, None),
            P("ctx", None, None),
            P(("groups", "ctx"), None),
            P(("groups", "ctx"), None),
        ),
        out_specs=(P(("groups", "ctx"), None), P(("groups", "ctx"), None)),
        check_vma=False,
    )
```

```python
import functools

import jax
import jax.numpy as jnp
from jax import lax
from jax.experimental import pallas as pl
from jax.experimental.pallas import tpu as pltpu
from jax.sharding import PartitionSpec as P

P_SIZE = 64
N = 64
GROUPS = 8
EXTRA = 16
MESH = pl.DeviceIdType.MESH
F32 = jnp.float32
BF16 = jnp.bfloat16


def ring_place(chips, chip):
    if chips == 8:
        z, y = chip // 2, chip % 2
        return z * (1 - y) + (7 - z) * y
    return chip


def ring_chip(chips, place):
    place = lax.rem(place + 2 * chips, chips)
    if chips == 8:
        back = place // 4
        return (1 - back) * (2 * place) + back * (2 * (7 - place) + 1)
    return place


def remote(src, dst, send, recv, device):
    return pltpu.make_async_remote_copy(
        src_ref=src,
        dst_ref=dst,
        send_sem=send,
        recv_sem=recv,
        device_id={"ctx": device},
        device_id_type=MESH,
    )


class Gather:
    def __init__(self, buf, chips, place, core, sems, skip=0, parity=0, partner=0):
        self.buf, self.chips, self.place, self.core = buf, chips, place, core
        self.half = chips // 2
        self.rows = buf.shape[1]
        self.skip, self.parity, self.partner = skip, parity, partner
        self.piece = (self.rows - skip) // 2
        self.ring_send, self.ring_recv, self.side_send, self.side_recv = sems[:4]
        self.cross = sems[4:]
        self.started = []

    def slot(self, place, core=None):
        return ring_chip(self.chips, place) * 2 + (self.core if core is None else core)

    def rows_at(self, place, start, count, core=None):
        return self.buf.at[self.slot(place, core), pl.ds(pl.multiple_of(start, 16), count)]

    def part(self, place, piece, core=None):
        return self.rows_at(place, self.parity * self.skip + piece * self.piece, self.piece, core)

    def pieces(self, way, step):
        return (way,) if step == self.half - 1 else (way, 1 - way)

    def index(self, way, step, piece):
        return (way * self.half + step) * 2 + piece

    def ring(self, way, step, piece):
        sign = 1 - 2 * way
        block = self.part(self.place - sign * (step + 1), piece)
        sem = self.index(way, step, piece)
        return remote(
            block, block, self.ring_send.at[sem], self.ring_recv.at[sem], self.slot(self.place + sign)
        )

    def side(self, index, block):
        return remote(
            block,
            block,
            self.side_send.at[index],
            self.side_recv.at[index],
            self.slot(self.place, 1 - self.core),
        )

    def go(self, copy):
        copy.start()
        self.started.append(copy)

    def send(self, way, step, piece):
        sign = 1 - 2 * way
        block = self.part(self.place - sign * step, piece)
        sem = self.index(way, step, piece)
        self.go(
            remote(
                block,
                block,
                self.ring_send.at[sem],
                self.ring_recv.at[sem],
                self.slot(self.place + sign),
            )
        )

    def start(self):
        for k in range(2):
            for way in range(2):
                self.send(way, 0, self.pieces(way, 0)[k])
        self.go(self.side(0, self.buf.at[self.slot(self.place)]))

    def far(self, step):
        if step == self.half - 1:
            return ((2 * step, self.place + self.half),)
        return tuple((2 * step + way, self.place - (1 - 2 * way) * (step + 1)) for way in range(2))

    def crossing(self, index, place, mine, core=None):
        start = (self.parity if mine else 1 - self.parity) * (self.rows - self.skip)
        block = self.rows_at(place, start, self.skip, core)
        if core is None:
            return pltpu.make_async_remote_copy(
                src_ref=block,
                dst_ref=block,
                send_sem=self.cross[0].at[index],
                recv_sem=self.cross[1].at[index],
                device_id={"groups": self.partner},
                device_id_type=MESH,
            )
        return remote(
            block,
            block,
            self.cross[2].at[index],
            self.cross[3].at[index],
            self.slot(self.place, 1 - self.core),
        )

    def step(self, step):
        for k in range(len(self.pieces(0, step))):
            for way in range(2):
                piece = self.pieces(way, step)[k]
                self.ring(way, step, piece).wait_recv()
                if step + 1 < self.half and piece in self.pieces(way, step + 1):
                    self.send(way, step + 1, piece)
                sign = 1 - 2 * way
                came = self.part(self.place - sign * (step + 1), piece)
                self.go(self.side(1 + self.index(way, step, piece), came))
        if self.skip:
            for index, place in self.far(step):
                self.go(self.crossing(index, place, True))
            if step:
                self.cross_step(step - 1)

    def cross_step(self, step):
        for index, place in self.far(step):
            self.crossing(index, place, False).wait_recv()
            self.go(self.crossing(index, place, False, self.core))

    def wait_side(self, step):
        other = 1 - self.core
        if step < 0:
            self.side(0, self.buf.at[self.slot(self.place, other)]).wait_recv()
            return
        for way in range(2):
            for piece in self.pieces(way, step):
                block = self.part(self.place - (1 - 2 * way) * (step + 1), piece, other)
                self.side(1 + self.index(way, step, piece), block).wait_recv()
        if self.skip:
            for index, place in self.far(step):
                self.crossing(index, place, False, other).wait_recv()

    def finish(self):
        for copy in self.started:
            copy.wait_send()
        self.started = []


def kernel(
    n,
    skip,
    values,
    in_b,
    out_c,
    decay_log,
    residual,
    mixer_gain,
    moe_gain,
    gates,
    w_down,
    w_in,
    w_out,
    mixed_out,
    mix_out,
    w_buf,
    lat_buf,
    *rest,
):
    chips = n // 2
    half = chips // 2
    apart = n <= 16
    if apart:
        parts, rest = rest[0], rest[1:]
    else:
        parts = lat_buf
    (
        y_buf,
        logs_t,
        normed,
        acc,
        st_send,
        st_recv,
        st_back,
        st_enter,
        before,
        tot_send,
        tot_recv,
        carry,
        gate_buf,
        win_buf,
        wout_buf,
        side_parts,
        sums,
        half_sums,
        local_sem,
        st_sem,
        st_rsem,
        back_sem,
        back_rsem,
        tot_sem,
        tot_rsem,
        gate_sem,
        gate_rsem,
        w_ring_s,
        w_ring_r,
        w_side_s,
        w_side_r,
        x_send,
        x_recv,
        x_side_s,
        x_side_r,
        l_ring_s,
        l_ring_r,
        l_side_s,
        l_side_r,
        p_side_s,
        p_side_r,
        s_send,
        s_recv,
    ) = rest
    me = lax.axis_index("ctx")
    core = lax.rem(me, 2)
    place = ring_place(chips, me // 2)
    tok = values.shape[0]
    width = values.shape[1] // n

    load_down = pltpu.make_async_copy(w_down, w_buf.at[me], local_sem.at[0])
    load_in = pltpu.make_async_copy(w_in.at[0], win_buf, local_sem.at[1])
    load_out = pltpu.make_async_copy(w_out.at[0], wout_buf, local_sem.at[2])
    load_down.start()
    load_in.start()
    load_out.start()

    barrier = pltpu.get_barrier_semaphore()

    @pl.loop(1, n)
    def _(i):
        pl.semaphore_signal(
            barrier, inc=1, device_id={"ctx": lax.rem(me + i, n)}, device_id_type=MESH
        )

    group = lax.axis_index("groups")
    parity = lax.rem(group, 2)
    partner = group + 1 - 2 * parity
    if skip:
        pl.semaphore_signal(
            barrier, inc=1, device_id={"groups": partner}, device_id_type=MESH
        )
    pl.semaphore_wait(barrier, n if skip else n - 1)
    load_down.wait()
    down = Gather(
        w_buf,
        chips,
        place,
        core,
        (w_ring_s, w_ring_r, w_side_s, w_side_r, x_send, x_recv, x_side_s, x_side_r),
        skip,
        parity,
        partner,
    )
    down.start()

    def gate_copy(to):
        return remote(gates.at[to], gate_buf.at[me], gate_sem.at[to], gate_rsem.at[me], to)

    row = lax.broadcasted_iota(jnp.int32, (tok, tok), 0)
    col = lax.broadcasted_iota(jnp.int32, (tok, tok), 1)
    lower = row >= col
    lower_f = lower.astype(F32)
    upper_f = (row <= col).astype(F32)
    left = lax.broadcasted_iota(jnp.int32, (tok, 128), 1) < P_SIZE
    left_row = left[:1]
    extra_row = lax.broadcasted_iota(jnp.int32, (EXTRA, 128), 0)

    def pair(a, b):
        return jnp.where(left, a, b)

    plane, quarter = me // 4, lax.rem(me, 4)
    planes = n // 4

    def st_copy(to):
        return remote(
            st_send.at[to], st_recv.at[quarter], st_sem.at[to], st_rsem.at[quarter], plane * 4 + to
        )

    @pl.loop(0, 4)
    def _(gp):
        logs = decay_log[pl.ds(pl.multiple_of(gp * 16, 16), 16), :]
        run = jnp.dot(logs, upper_f, precision=lax.Precision.HIGHEST, preferred_element_type=F32)
        run_t = lax.dot_general(
            lower_f,
            logs,
            (((1,), (1,)), ((), ())),
            precision=lax.Precision.HIGHEST,
            preferred_element_type=F32,
        )
        logs_t[gp] = run_t
        tails = jnp.exp(run_t[tok - 1 : tok, :] - run_t)
        total = jnp.exp(run_t[tok - 1 : tok, :])
        two = pl.ds(pl.multiple_of(gp * 128, 128), 128)
        b2, c2 = in_b[:, two], out_c[:, two]
        for gi in range(2):
            b = b2[:, gi * N : (gi + 1) * N]
            c = c2[:, gi * N : (gi + 1) * N]
            scores = lax.dot_general(c, b, (((1,), (1,)), ((), ())), preferred_element_type=F32)
            for hp in range(4):
                h = gi * 8 + hp * 2
                cols = pl.ds(pl.multiple_of(gp * 1024 + gi * 512 + hp * 128, 128), 128)
                v = values[:, cols]
                weights = []
                for k in range(2):
                    spread = run_t[:, h + k : h + k + 1] - run[h + k : h + k + 1, :]
                    decays = jnp.exp(jnp.where(lower, spread, -1e30))
                    weights.append((scores * decays).astype(BF16))
                zero = jnp.zeros_like(v)
                stacked = jnp.concatenate([pair(v, zero), pair(zero, v)], axis=0)
                y_buf[:, cols] = jnp.dot(
                    jnp.concatenate(weights, axis=1), stacked, preferred_element_type=F32
                )
                tail = pair(tails[:, h : h + 1], tails[:, h + 1 : h + 2])
                scaled = (v.astype(F32) * tail).astype(BF16)
                update = lax.dot_general(
                    b, scaled, (((0,), (0,)), ((), ())), preferred_element_type=F32
                ).astype(BF16)
                dec = jnp.where(left_row, total[:, h : h + 1], total[:, h + 1 : h + 2])
                high = dec.astype(BF16).astype(F32)
                mid = (dec - high).astype(BF16).astype(F32)
                low = dec - high - mid
                extra = jnp.where(
                    extra_row == 0, high, jnp.where(extra_row == 1, mid, low)
                ).astype(BF16)
                at = gi * 512 + hp * 128
                st_send[gp, :N, at : at + 128] = update
                st_send[gp, N:, at : at + 128] = extra

        @pl.when(gp != quarter)
        def _():
            st_copy(gp).start()

        @pl.when(gp == quarter)
        def _():
            st_recv[quarter] = st_send[quarter]

    def take(block):
        block = block.astype(F32)
        return block[N : N + 1] + block[N + 1 : N + 2] + block[N + 2 : N + 3], block[:N]

    state = jnp.zeros((N, 1024), F32)
    total = jnp.ones((1, 1024), F32)
    for i in range(4):

        @pl.when(quarter != i)
        def _():
            remote(
                st_send.at[i], st_recv.at[i], st_sem.at[i], st_rsem.at[i], plane * 4 + i
            ).wait_recv()

        before[i, :N] = state
        before[i, N : N + 8] = jnp.broadcast_to(total, (8, 1024))
        dec, update = take(st_recv[i])
        state = dec * state + update
        total = dec * total
    high = total.astype(BF16).astype(F32)
    mid = (total - high).astype(BF16).astype(F32)
    place_row = lax.broadcasted_iota(jnp.int32, (EXTRA, 1024), 0)
    tot_send[:N] = state.astype(BF16)
    tot_send[N:] = jnp.where(
        place_row == 0, high, jnp.where(place_row == 1, mid, total - high - mid)
    ).astype(BF16)

    def tot_copy(to):
        return remote(
            tot_send, tot_recv.at[plane], tot_sem.at[to], tot_rsem.at[plane], to * 4 + quarter
        )

    @pl.loop(0, planes)
    def _(to):
        @pl.when(to > plane)
        def _():
            tot_copy(to).start()

    down.step(0)

    @pl.loop(1, n)
    def _(i):
        gate_copy(lax.rem(me + i, n)).start()

    gate_buf[me] = gates[me]

    carry[...] = jnp.zeros_like(carry)

    @pl.loop(0, planes)
    def _(i):
        @pl.when(i < plane)
        def _():
            remote(
                tot_send, tot_recv.at[i], tot_sem.at[i], tot_rsem.at[i], i * 4 + quarter
            ).wait_recv()
            dec, update = take(tot_recv[i])
            carry[...] = dec * carry[...] + update

    def back_copy(to):
        return remote(
            st_back.at[to], st_enter.at[quarter], back_sem.at[to], back_rsem.at[quarter], plane * 4 + to
        )

    for i in range(4):
        st_back[i] = (before[i, :N] + before[i, N : N + 1] * carry[...]).astype(BF16)

        @pl.when(quarter != i)
        def _():
            back_copy(i).start()

        @pl.when(quarter == i)
        def _():
            st_enter[quarter] = st_back[quarter]

    for step in range(1, half - 2):
        down.step(step)

    @pl.loop(1, 4)
    def _(i):
        src = lax.rem(quarter + i, 4)
        remote(
            st_back.at[src],
            st_enter.at[src],
            back_sem.at[src],
            back_rsem.at[src],
            plane * 4 + src,
        ).wait_recv()

    def finish_mixer(gp, squares):
        reach_scale = jnp.exp(logs_t[gp])
        c2 = out_c[:, pl.ds(pl.multiple_of(gp * 128, 128), 128)]
        for gi in range(2):
            c = c2[:, gi * N : (gi + 1) * N]
            for hp in range(4):
                h = gi * 8 + hp * 2
                cols = pl.ds(pl.multiple_of(gp * 1024 + gi * 512 + hp * 128, 128), 128)
                at = gi * 512 + hp * 128
                enter = st_enter[gp, :, at : at + 128]
                reach = jnp.dot(c, enter, preferred_element_type=F32)
                y = y_buf[:, cols] + pair(reach_scale[:, h : h + 1], reach_scale[:, h + 1 : h + 2]) * reach
                square = y * y
                both = jnp.sum(square, axis=1, keepdims=True)
                one = jnp.sum(jnp.where(left, square, 0.0), axis=1, keepdims=True)
                other = jnp.sum(jnp.where(left, 0.0, square), axis=1, keepdims=True)
                del both
                scale = pair(
                    lax.rsqrt(one * (1.0 / P_SIZE) + 1e-05),
                    lax.rsqrt(other * (1.0 / P_SIZE) + 1e-05),
                )
                mixed = (
                    residual[:, cols].astype(F32) + y * scale * mixer_gain[:, cols]
                ).astype(BF16)
                mixed_out[:, cols] = mixed
                wide = mixed.astype(F32)
                squares = squares + wide * wide
        return squares

    squares = lax.fori_loop(0, 4, finish_mixer, jnp.zeros((tok, 128), F32))
    mean = jnp.sum(squares, axis=1, keepdims=True) * (1.0 / (n * width))
    row_scale = lax.rsqrt(mean + 1e-05)
    rows = w_buf.shape[1]
    if rows >= 128:

        @pl.loop(0, n)
        def _(i):
            cols = pl.ds(pl.multiple_of(i * rows, rows), rows)
            wide = mixed_out[:, cols].astype(F32)
            normed[i] = (wide * row_scale * moe_gain[:, cols]).astype(BF16)
    else:

        @pl.loop(0, n // 2)
        def _(i):
            cols = pl.ds(pl.multiple_of(i * 128, 128), 128)
            wide = mixed_out[:, cols].astype(F32)
            both = (wide * row_scale * moe_gain[:, cols]).astype(BF16)
            normed[2 * i] = both[:, :rows]
            normed[2 * i + 1] = both[:, rows:]

    for step in range(half - 2, half):
        down.step(step)
    for step in range(-1, half - 1):
        down.wait_side(step)
    acc[...] = jnp.zeros_like(acc)

    def project(place_of):
        chip = ring_chip(chips, place_of)
        for k in range(2):
            slot = 2 * chip + k
            acc[...] += jnp.dot(normed[slot], w_buf[slot], preferred_element_type=F32)

    @pl.loop(0, chips - 1)
    def _(i):
        project(place + i + i // half)

    if skip:
        down.cross_step(half - 1)
    down.wait_side(half - 1)
    project(place + half)
    lat_buf[me] = acc[...].astype(BF16)

    lat = Gather(lat_buf, chips, place, core, (l_ring_s, l_ring_r, l_side_s, l_side_r))
    lat.start()

    @pl.loop(1, n)
    def _(i):
        src = lax.rem(me + i, n)
        remote(
            gates.at[src], gate_buf.at[src], gate_sem.at[src], gate_rsem.at[src], src
        ).wait_recv()

    load_in.wait()
    load_out.wait()

    def expert(place_of):
        chip = ring_chip(chips, place_of)
        x = lat_buf[pl.ds(2 * chip, 2)].reshape(2 * tok, lat_buf.shape[2])
        hidden = jnp.dot(x, win_buf[...], preferred_element_type=F32)
        hidden = jnp.square(jnp.maximum(hidden, 0.0)).astype(BF16)
        out = jnp.dot(hidden, wout_buf[...], preferred_element_type=F32).astype(BF16).astype(F32)
        for k in range(2):
            gate = jnp.transpose(gate_buf[2 * chip + k])[:, :1]
            parts[2 * chip + k] = (out[k * tok : (k + 1) * tok] * gate).astype(BF16)

    def part_copy(index, place_of):
        chip = ring_chip(chips, place_of)
        return remote(
            parts.at[2 * chip + 1 - core],
            side_parts.at[chip],
            p_side_s.at[index],
            p_side_r.at[index],
            ring_chip(chips, place) * 2 + 1 - core,
        )

    def work(step):
        if step < 0:
            expert(place)
            part_copy(0, place).start()
        elif step == half - 1:
            expert(place + half)
            part_copy(2 * half - 1, place + half).start()
        else:

            @pl.loop(0, 2)
            def _(way):
                there = place - (1 - 2 * way) * (step + 1)
                expert(there)
                part_copy(1 + 2 * step + way, there).start()

    if apart:
        for step in range(half):
            lat.step(step)
            lat.wait_side(step - 1)
            work(step - 1)
        lat.wait_side(half - 1)
        work(half - 1)
        lat.finish()
    else:
        for step in range(half):
            lat.step(step)
        for step in range(-1, half):
            lat.wait_side(step)
        lat.finish()
        for step in range(-1, half):
            work(step)

    def pair_sum(index, place_of):
        chip = ring_chip(chips, place_of)
        part_copy(index, place_of).wait_recv()
        slot = 2 * chip + core
        parts[slot] = (parts[slot].astype(F32) + side_parts[chip].astype(F32)).astype(BF16)

    cut = tok // 2

    def sum_copy(way, step, piece):
        sign = 1 - 2 * way
        there = place + sign * (half - step)
        some = pl.ds(piece * cut, cut)
        block = parts.at[2 * ring_chip(chips, there) + core, some]
        to = ring_chip(chips, place + sign) * 2 + core
        if step == 0:
            target = half_sums.at[way]
        else:
            target = sums.at[way * (half - 1) + step - 1, some]
        sem = (way * half + step) * 2 + piece
        return remote(block, target, s_send.at[sem], s_recv.at[sem], to)

    sent = []

    def send_sum(way, step, piece):
        sent.append(sum_copy(way, step, piece))
        sent[-1].start()

    pair_sum(2 * half - 1, place + half)
    for way in range(2):
        send_sum(way, 0, way)
    for step in range(1, half):
        for way in range(2):
            there = place + (1 - 2 * way) * (half - step)
            pair_sum(1 + 2 * (half - step - 1) + (1 - way), there)
        for first in (True, False):
            for way in range(2):
                piece = 1 - way if first else way
                there = place + (1 - 2 * way) * (half - step)
                slot = 2 * ring_chip(chips, there) + core
                some = pl.ds(piece * cut, cut)
                if step > 1 or not first:
                    sum_copy(way, step - 1, piece).wait_recv()
                    if step == 1:
                        came = half_sums[way]
                    else:
                        came = sums[way * (half - 1) + step - 2, some]
                    parts[slot, some] = (
                        parts[slot, some].astype(F32) + came.astype(F32)
                    ).astype(BF16)
                send_sum(way, step, piece)
    part_copy(0, place).wait_recv()
    mine = ring_chip(chips, place)
    whole = parts[2 * mine + core].astype(F32) + side_parts[mine].astype(F32)
    for way in range(2):
        for piece in range(2):
            sum_copy(way, half - 1, piece).wait_recv()
        whole = whole + sums[way * (half - 1) + half - 2].astype(F32)
    mix_out[...] = whole.astype(BF16)

    for copy in sent:
        copy.wait_send()
    for index in range(2 * half):
        part_copy(index, place).wait_send()
    down.finish()

    @pl.loop(1, n)
    def _(i):
        to = lax.rem(me + i, n)
        gate_copy(to).wait_send()

    @pl.loop(1, 4)
    def _(i):
        to = lax.rem(quarter + i, 4)
        st_copy(to).wait_send()
        back_copy(to).wait_send()

    @pl.loop(0, planes)
    def _(to):
        @pl.when(to > plane)
        def _():
            tot_copy(to).wait_send()


def on_device(
    values,
    in_b,
    out_c,
    decay_log,
    residual,
    mixer_gain,
    moe_gain,
    w_down,
    w_in,
    w_out,
    routes,
    gate_int,
):
    n = lax.axis_size("ctx")
    tok, width = values.shape
    latent = w_down.shape[1]
    chips = n // 2
    half = chips // 2
    gate_float = gate_int.astype(F32)
    gate = gate_float / jnp.sum(gate_float, axis=1, keepdims=True)
    named = routes[None] == jnp.arange(n, dtype=jnp.int32)[:, None, None]
    table = jnp.sum(jnp.where(named, gate[None], 0.0), axis=2)
    gates = jnp.broadcast_to(table[:, None, :], (n, 8, tok))
    vmem = pl.BlockSpec(memory_space=pltpu.VMEM)
    anywhere = pl.BlockSpec(memory_space=pl.ANY)
    dma = lambda count: pltpu.SemaphoreType.DMA((count,))
    scratch = [
        pltpu.VMEM((n,) + w_down.shape, BF16),
        pltpu.VMEM((n, tok, latent), BF16),
    ]
    if n <= 16:
        scratch.append(pltpu.VMEM((n, tok, latent), BF16))
    scratch += [
        pltpu.VMEM((tok, width), F32),
        pltpu.VMEM((4, tok, 16), F32),
        pltpu.VMEM((n, tok, w_down.shape[0]), BF16),
        pltpu.VMEM((tok, latent), F32),
        pltpu.VMEM((4, N + EXTRA, 1024), BF16),
        pltpu.VMEM((4, N + EXTRA, 1024), BF16),
        pltpu.VMEM((4, N, 1024), BF16),
        pltpu.VMEM((4, N, 1024), BF16),
        pltpu.VMEM((4, N + 8, 1024), F32),
        pltpu.VMEM((N + EXTRA, 1024), BF16),
        pltpu.VMEM((n // 4, N + EXTRA, 1024), BF16),
        pltpu.VMEM((N, 1024), F32),
        pltpu.VMEM((n, 8, tok), F32),
        pltpu.VMEM(w_in.shape[1:], BF16),
        pltpu.VMEM(w_out.shape[1:], BF16),
        pltpu.VMEM((chips, tok, latent), BF16),
        pltpu.VMEM((2 * (half - 1), tok, latent), BF16),
        pltpu.VMEM((2, tok // 2, latent), BF16),
        dma(3),
    ]
    scratch += [dma(4)] * 4 + [dma(n // 4)] * 2 + [dma(n)] * 2
    ring = [dma(4 * half)] * 2 + [dma(4 * half + 1)] * 2
    scratch += ring + [dma(2 * half)] * 4 + ring
    scratch += [dma(2 * half)] * 2 + [dma(4 * half)] * 2
    skip = w_down.shape[0] // 4 // 32 * 32 if lax.axis_size("groups") % 2 == 0 else 0
    return pl.pallas_call(
        functools.partial(kernel, n, skip),
        out_shape=(
            jax.ShapeDtypeStruct((tok, width), BF16),
            jax.ShapeDtypeStruct((tok, latent), BF16),
        ),
        in_specs=[vmem] * 8 + [anywhere] * 3,
        out_specs=(vmem, vmem),
        scratch_shapes=scratch,
        compiler_params=pltpu.CompilerParams(
            collective_id=0, has_side_effects=True, vmem_limit_bytes=62 * 1024 * 1024
        ),
    )(
        values,
        in_b,
        out_c,
        decay_log,
        residual,
        mixer_gain.reshape(1, -1),
        moe_gain.reshape(1, -1),
        gates,
        w_down,
        w_in,
        w_out,
    )


def solution(mesh):
    return jax.shard_map(
        on_device,
        mesh=mesh,
        in_specs=(
            P(("groups", "ctx"), None),
            P(("groups", "ctx"), None),
            P(("groups", "ctx"), None),
            P(None, ("groups", "ctx")),
            P(("groups", "ctx"), None),
            P(),
            P(),
            P("ctx", None),
            P("ctx", None, None),
            P("ctx", None, None),
            P(("groups", "ctx"), None),
            P(("groups", "ctx"), None),
        ),
        out_specs=(P(("groups", "ctx"), None), P(("groups", "ctx"), None)),
        check_vma=False,
    )
```
